256 devices in a mesh: seq: 8 (over z_hi, x), res: 32 (over z_lo, y, core).
Axes of the slice: x: 4, y: 4, z: 8 (z_hi: 2, z_lo: 4; z = z_hi * 4 + z_lo), core: 2. Of those that a mesh axis runs over, the one named last changes fastest.
Arguments:
- alignment_embeddings: bfloat16 [64, 1024, 768], P('seq', 'res'), may hold values from -6 to 6
- standardize_gain: float32 [768], replicated, may hold values from 0.5 to 1.5
- asking_projection: bfloat16 [768, 768], replicated
- lookup_projection: bfloat16 [768, 768], replicated, may hold values from -0.21875 to 0.21875
- content_projection: bfloat16 [768, 768], replicated, may hold values from -0.21875 to 0.21875
- final_projection: bfloat16 [768, 768], replicated, may hold values from -0.21875 to 0.21875
Outputs:
- updated: bfloat16 [64, 1024, 768], P('seq', 'res')
The draws below stay inside these ranges and needn't reach their ends.
All inputs are finite; a program needn't handle non-finite values.
Results may differ from the reference program's by a relative error of at most 0.012.
The reference program's roundings to bfloat16 on the way (of `normed`, `probs` and `context`) count: a program that leaves them out, or rounds other values in their place, can miss the bound.
Values may be sent and summed in bfloat16 or wider, within the bound.
No kernel may reach another device: no remote copies, remote signals or barrier semaphores. Data moves between devices by JAX's collectives and lax.ppermute only.
A program may use at most 128 MiB of HBM per device.

```python
import math
import jax
import jax.numpy as jnp
from jax import lax

EMBED_DIMENSION = 768
HEADS = 12
HEAD_SIZE = 64
ALIGNED_TOTAL = 64
POSITION_TOTAL = 1024


def draw_asking_projection(key, part):
    key = jax.random.fold_in(key, 11)
    first = jax.random.fold_in(key, 0)
    base = jax.random.normal(first, (EMBED_DIMENSION, EMBED_DIMENSION), jnp.float32)
    return (base * (3.0 / math.sqrt(EMBED_DIMENSION))).astype(jnp.bfloat16)


def steps_of(key, dims, cuts, least, largest):
    level, own = 1.0, jax.random.fold_in(key, 6)
    for axis_at, parts in cuts:
        steps = jnp.exp(jax.random.uniform(jax.random.fold_in(own, axis_at), (parts,), jnp.float32, least / len(cuts), largest / len(cuts)))
        level = level * jnp.repeat(steps, dims[axis_at] // parts).reshape([-1 if axis == axis_at else 1 for axis in range(len(dims))])
    return level


def normal_values(key, dims, width, most, shards=(), kind=jnp.bfloat16):
    gain = steps_of(key, dims, shards, -0.22, 0.18) if shards else 1.0
    array = jax.random.normal(key, dims, jnp.float32) * width * gain
    return jnp.minimum(jnp.maximum(array, -most), most).astype(kind)


def setup_inputs(seed: int = 0) -> dict:
    key_of = jax.random.split(jax.random.key(seed), 7)
    alignment_embeddings = normal_values(key_of[0], (ALIGNED_TOTAL, POSITION_TOTAL, EMBED_DIMENSION), 1.0, 6.0, ((0, 8), (1, 32)))
    standardize_gain = jnp.clip(jax.random.uniform(key_of[1], (EMBED_DIMENSION,), jnp.float32, 0.5, 1.5), 0.5, 1.5)
    asking_projection = draw_asking_projection(jax.random.fold_in(key_of[6], 71), 0)
    lookup_projection = normal_values(key_of[3], (EMBED_DIMENSION, EMBED_DIMENSION), EMBED_DIMENSION ** -0.5, 0.21875)
    content_projection = normal_values(key_of[4], (EMBED_DIMENSION, EMBED_DIMENSION), EMBED_DIMENSION ** -0.5, 0.21875)
    final_projection = normal_values(key_of[5], (EMBED_DIMENSION, EMBED_DIMENSION), EMBED_DIMENSION ** -0.5, 0.21875)
    return {"alignment_embeddings": alignment_embeddings, "standardize_gain": standardize_gain, "asking_projection": asking_projection, "lookup_projection": lookup_projection, "content_projection": content_projection, "final_projection": final_projection}


def reference(alignment_embeddings, standardize_gain, asking_projection, lookup_projection, content_projection, final_projection):
    alignment_member, column_position, embed_dimension = alignment_embeddings.shape
    broad_arrangement = alignment_embeddings.astype(jnp.float32)
    mean = lax.optimization_barrier(jnp.mean(broad_arrangement, axis=-1, keepdims=True))
    var = lax.optimization_barrier(jnp.mean((broad_arrangement - mean) ** 2, axis=-1, keepdims=True))
    normed = ((broad_arrangement - mean) / jnp.sqrt(var + 1e-05) * standardize_gain).astype(jnp.bfloat16)
    flat = normed.reshape(alignment_member * column_position, embed_dimension)
    query = jnp.dot(flat, asking_projection, preferred_element_type=jnp.float32).astype(jnp.bfloat16)
    key = jnp.dot(flat, lookup_projection, preferred_element_type=jnp.float32).astype(jnp.bfloat16)
    value = jnp.dot(flat, content_projection, preferred_element_type=jnp.float32).astype(jnp.bfloat16)
    query = query.reshape(alignment_member, column_position, HEADS, HEAD_SIZE).astype(jnp.float32)
    key = key.reshape(alignment_member, column_position, HEADS, HEAD_SIZE).astype(jnp.float32)
    value = value.reshape(alignment_member, column_position, HEADS, HEAD_SIZE).astype(jnp.float32)
    scale = HEAD_SIZE ** (-0.5) / jnp.sqrt(jnp.float32(alignment_member))
    logits = jnp.einsum('sihd,sjhd->hij', query, key) * scale
    probs = jax.nn.softmax(logits, axis=-1).astype(jnp.bfloat16)
    context = jnp.einsum('hij,sjhd->sihd', probs.astype(jnp.float32), value).astype(jnp.bfloat16)
    mixed = jnp.dot(context.reshape(alignment_member * column_position, embed_dimension), final_projection, preferred_element_type=jnp.float32)
    return (broad_arrangement + mixed.reshape(alignment_member, column_position, embed_dimension)).astype(jnp.bfloat16)
```

```python
import functools

import jax
import jax.numpy as jnp
from jax import lax
from jax.experimental import pallas as pl
from jax.experimental.pallas import tpu as pltpu
from jax.sharding import Mesh
from jax.sharding import PartitionSpec as P

HEADS = 12
SIZE = 64
GROUPS = 4
OWN = HEADS // GROUPS
F32, BF16 = jnp.float32, jnp.bfloat16
LINE = [[(i, i ^ m) for i in range(4)] for m in range(4)]
RING = [[(i, (i + k) % 4) for i in range(4)] for k in range(4)]
VMEM = pl.BlockSpec(memory_space=pltpu.VMEM)
LIMIT = 48 * 1024 * 1024


def call(body, outs, scratch=(), flops=1000000, moved=1000000):
    def run(*args):
        return pl.pallas_call(
            body,
            out_shape=[jax.ShapeDtypeStruct(s, d) for s, d in outs],
            in_specs=[VMEM] * len(args),
            out_specs=[VMEM] * len(outs),
            scratch_shapes=list(scratch),
            compiler_params=pltpu.CompilerParams(vmem_limit_bytes=LIMIT),
            cost_estimate=pl.CostEstimate(
                flops=flops, bytes_accessed=moved, transcendentals=0
            ),
        )(*args)

    return run


def pack(full, store):
    parts = full.reshape(4, 2, 32, HEADS * SIZE)
    even, odd = parts[:, 0].reshape(128, -1), parts[:, 1].reshape(128, -1)
    for n in range(HEADS // 2):
        a, b = even[:, n * 128 : n * 128 + 128], odd[:, n * 128 : n * 128 + 128]
        store(2 * n, jnp.concatenate([a[:, :64], b[:, :64]], axis=1).astype(BF16))
        store(2 * n + 1, jnp.concatenate([a[:, 64:], b[:, 64:]], axis=1).astype(BF16))


def key_kernel(x_ref, gain_ref, w_ref, normed_ref, o0, o1, o2, o3, held):
    x = x_ref[...].astype(F32)
    mean = jnp.mean(x, axis=-1, keepdims=True)
    off = x - mean
    var = jnp.mean(off * off, axis=-1, keepdims=True)
    normed = (off / jnp.sqrt(var + 1e-05) * gain_ref[...]).astype(BF16)
    normed_ref[...] = normed
    full = jnp.dot(normed, w_ref[...], preferred_element_type=F32)

    def store(h, block):
        held[h // OWN, (h % OWN) * 128 : (h % OWN) * 128 + 128, :] = block

    pack(full, store)
    me = lax.axis_index("zl")
    for m, out in enumerate((o0, o1, o2, o3)):
        out[...] = held[jnp.bitwise_xor(me, m)]


def query_value_kernel(normed_ref, wq_ref, wv_ref, o0, o1, o2, o3, held):
    normed = normed_ref[...]
    for part, w_ref in enumerate((wq_ref, wv_ref)):
        full = jnp.dot(normed, w_ref[...], preferred_element_type=F32)

        def store(h, block, part=part):
            row = part * 384 + (h % OWN) * 128
            held[h // OWN, row : row + 128, :] = block

        pack(full, store)
    me = lax.axis_index("zl")
    for m, out in enumerate((o0, o1, o2, o3)):
        out[...] = held[jnp.bitwise_xor(me, m)]


def slab_kernel(base, p0, p1, p2, p3, slab):
    for m, piece in enumerate((p0, p1, p2, p3)):
        for h in range(OWN):
            for sp in range(4):
                row = base + h * 128 + sp * 32
                slab[h * 128 + m * 32 : h * 128 + m * 32 + 32, sp * 128 : sp * 128 + 128] = (
                    piece[row : row + 32, :]
                )


def logits_kernel(*refs):
    pieces, slabs = refs[:4], refs[4:12]
    own, others, held = refs[12], refs[13:16], refs[16]
    me = lax.axis_index("x")
    for m, piece in enumerate(pieces):
        at = lax.rem(m - me + 4, 4)
        for h in range(OWN):
            for sp in range(4):
                row = h * 128 + sp * 32
                held[h, at, :, sp * 128 : sp * 128 + 128] = piece[row : row + 32, :]
    for h in range(OWN):
        query = held[h].reshape(128, 512)
        for j, slab in enumerate(slabs):
            part = lax.dot_general(
                query,
                slab[h * 128 : h * 128 + 128, :],
                (((1,), (1,)), ((), ())),
                preferred_element_type=F32,
            )
            cols = slice(j * 128, j * 128 + 128)
            own[h * 32 : h * 32 + 32, cols] = part[:32]
            for k, out in enumerate(others):
                out[h * 32 : h * 32 + 32, cols] = part[k * 32 + 32 : k * 32 + 64].astype(BF16)


def sum_kernel(own, r1, r2, r3, total, sent):
    s = own[...] + r1[...].astype(F32) + r2[...].astype(F32) + r3[...].astype(F32)
    total[...] = s
    sent[...] = s.astype(BF16)


def softmax_kernel(scale, total, other, probs):
    logits = (total[...] + other[...].astype(F32)) * scale
    top = jnp.max(logits, axis=-1, keepdims=True)
    e = jnp.exp(logits - top)
    probs[...] = (e / jnp.sum(e, axis=-1, keepdims=True)).astype(BF16)


def context_kernel(*refs):
    probs, slabs, outs, held = refs[:4], refs[4:12], refs[12:16], refs[16]
    me = lax.axis_index("x")
    for k, piece in enumerate(probs):
        at = lax.rem(me - k + 4, 4)
        for h in range(OWN):
            held[h, at] = piece[h * 32 : h * 32 + 32, :]
    for h in range(OWN):
        p = held[h].reshape(128, 1024)
        total = None
        for j, slab in enumerate(slabs):
            part = jnp.dot(
                p[:, j * 128 : j * 128 + 128],
                slab[h * 128 : h * 128 + 128, :],
                preferred_element_type=F32,
            )
            total = part if total is None else total + part
        total = total.astype(BF16)
        for m, out in enumerate(outs):
            for sp in range(4):
                row = h * 128 + sp * 32
                out[row : row + 32, :] = total[
                    m * 32 : m * 32 + 32, sp * 128 : sp * 128 + 128
                ]


def out_kernel(c0, c1, c2, c3, x_ref, w_ref, out, held, context):
    me = lax.axis_index("zl")
    for m, piece in enumerate((c0, c1, c2, c3)):
        held[jnp.bitwise_xor(me, m)] = piece[...]

    def block(h):
        return held[h // OWN, (h % OWN) * 128 : (h % OWN) * 128 + 128, :].astype(F32)

    for n in range(HEADS // 2):
        a, b = block(2 * n), block(2 * n + 1)
        even = jnp.concatenate([a[:, :64], b[:, :64]], axis=1).astype(BF16)
        odd = jnp.concatenate([a[:, 64:], b[:, 64:]], axis=1).astype(BF16)
        for sp in range(4):
            rows = slice(sp * 32, sp * 32 + 32)
            cols = slice(n * 128, n * 128 + 128)
            context[sp * 64 : sp * 64 + 32, cols] = even[rows]
            context[sp * 64 + 32 : sp * 64 + 64, cols] = odd[rows]
    mixed = jnp.dot(context[...], w_ref[...], preferred_element_type=F32)
    out[...] = (x_ref[...].astype(F32) + mixed).astype(BF16)


def line(pieces):
    return (pieces[0], *(lax.ppermute(pieces[m], "zl", LINE[m]) for m in (1, 2, 3)))


def around(slab):
    ring = [slab] + [lax.ppermute(slab, "y", RING[k]) for k in (1, 3, 2)]
    return ring + [lax.ppermute(s, "c", [(0, 1), (1, 0)]) for s in ring]


def per_device(x, gain, wq, wk, wv, wf):
    flat = x.reshape(256, 768)
    piece = ((384, 128), BF16)
    both = ((768, 128), BF16)
    slab = [((384, 512), BF16)]
    part = ((96, 1024), BF16)
    normed, *keys = call(
        key_kernel, [((256, 768), BF16)] + [piece] * 4, [pltpu.VMEM((4, 384, 128), BF16)]
    )(flat, gain.reshape(1, 768), wk)
    pairs = call(query_value_kernel, [both] * 4, [pltpu.VMEM((4, 768, 128), BF16)])(
        normed, wq, wv
    )
    keys = line(keys)
    keys, pairs = lax.optimization_barrier((tuple(keys), tuple(pairs)))
    (key_slab,) = call(functools.partial(slab_kernel, 0), slab)(*keys)
    pairs = line(pairs)
    key_slabs = around(key_slab)
    own, *others = call(
        logits_kernel,
        [((96, 1024), F32)] + [part] * 3,
        [pltpu.VMEM((OWN, 4, 32, 512), BF16)],
    )(*pairs, *key_slabs)
    (value_slab,) = call(functools.partial(slab_kernel, 384), slab)(*pairs)
    value_slabs = around(value_slab)
    got = [lax.ppermute(others[k - 1], "x", RING[k]) for k in (1, 2, 3)]
    total, sent = call(sum_kernel, [((96, 1024), F32), part])(own, *got)
    other = lax.ppermute(sent, "zh", [(0, 1), (1, 0)])
    scale = SIZE ** (-0.5) / (64.0**0.5)
    (probs,) = call(functools.partial(softmax_kernel, scale), [part])(total, other)
    probs = [probs] + [lax.ppermute(probs, "x", RING[k]) for k in (1, 2, 3)]
    context = call(
        context_kernel, [piece] * 4, [pltpu.VMEM((OWN, 4, 32, 1024), BF16)]
    )(*probs, *value_slabs)
    context = line(context)
    (out,) = call(
        out_kernel,
        [((256, 768), BF16)],
        [pltpu.VMEM((4, 384, 128), BF16), pltpu.VMEM((256, 768), BF16)],
    )(*context, flat, wf)
    return out.reshape(8, 32, 768)


def solution(mesh):
    fine = Mesh(mesh.devices.reshape(2, 4, 4, 4, 2), ("zh", "x", "zl", "y", "c"))
    split = P(("zh", "x"), ("zl", "y", "c"), None)
    return jax.shard_map(
        per_device,
        mesh=fine,
        in_specs=(split, P(), P(), P(), P(), P()),
        out_specs=split,
        check_vma=False,
    )
```

```python
import functools

import jax
import jax.numpy as jnp
from jax import lax
from jax.experimental import pallas as pl
from jax.experimental.pallas import tpu as pltpu
from jax.sharding import Mesh
from jax.sharding import PartitionSpec as P

HEADS = 12
SIZE = 64
GROUPS = 4
OWN = HEADS // GROUPS
F32, BF16 = jnp.float32, jnp.bfloat16
LINE = [[(i, i ^ m) for i in range(4)] for m in range(4)]
RING = [[(i, (i + k) % 4) for i in range(4)] for k in range(4)]
VMEM = pl.BlockSpec(memory_space=pltpu.VMEM)
FAR = pl.BlockSpec(memory_space=pltpu.HBM)
LIMIT = 48 * 1024 * 1024
MOST = 60 * 1024 * 1024


def call(body, outs, scratch=(), flops=5000000000, moved=1000000, places=None, after=(), limit=LIMIT):
    def run(*args):
        count = len(args)

        def kernel(*refs):
            body(*refs[:count], *refs[count + len(after) :])

        specs = [places.get(i, VMEM) if places else VMEM for i in range(count)]
        return pl.pallas_call(
            kernel,
            out_shape=[jax.ShapeDtypeStruct(s, d) for s, d in outs],
            in_specs=specs + [FAR] * len(after),
            out_specs=[VMEM] * len(outs),
            scratch_shapes=list(scratch),
            compiler_params=pltpu.CompilerParams(vmem_limit_bytes=limit),
            cost_estimate=pl.CostEstimate(
                flops=flops, bytes_accessed=moved, transcendentals=0
            ),
        )(*args, *after)

    return run


def pack(full, store):
    parts = full.reshape(4, 2, 32, HEADS * SIZE)
    even, odd = parts[:, 0].reshape(128, -1), parts[:, 1].reshape(128, -1)
    for n in range(HEADS // 2):
        a, b = even[:, n * 128 : n * 128 + 128], odd[:, n * 128 : n * 128 + 128]
        store(2 * n, jnp.concatenate([a[:, :64], b[:, :64]], axis=1).astype(BF16))
        store(2 * n + 1, jnp.concatenate([a[:, 64:], b[:, 64:]], axis=1).astype(BF16))


def key_kernel(x_far, gain_far, w_far, normed_ref, o0, o1, o2, o3, held, x_ref, gain_ref, w_ref, sems):
    copies = [
        pltpu.make_async_copy(far, near, sems.at[i])
        for i, (far, near) in enumerate(
            ((x_far, x_ref), (gain_far, gain_ref), (w_far, w_ref))
        )
    ]
    for copy in copies:
        copy.start()
    copies[0].wait()
    x = x_ref[...].astype(F32)
    mean = jnp.mean(x, axis=-1, keepdims=True)
    off = x - mean
    var = jnp.mean(off * off, axis=-1, keepdims=True)
    copies[1].wait()
    gain = gain_ref[...].reshape(1, HEADS * SIZE)
    normed = (off / jnp.sqrt(var + 1e-05) * gain).astype(BF16)
    normed_ref[...] = normed
    copies[2].wait()
    spread(normed, w_ref, (o0, o1, o2, o3), held)


def spread(normed, w_ref, outs, held, row=0):
    full = jnp.dot(normed, w_ref[...], preferred_element_type=F32)

    def store(h, block):
        held[h // OWN, (h % OWN) * 128 : (h % OWN) * 128 + 128, :] = block

    pack(full, store)
    me = lax.axis_index("zl")
    for m, out in enumerate(outs):
        out[row : row + 384, :] = held[jnp.bitwise_xor(me, m)]


def projection_kernel(normed_ref, *refs):
    n = (len(refs) - 5)
    outs, held = refs[n:-1], refs[-1]
    for i, w_ref in enumerate(refs[:n]):
        spread(normed_ref[...], w_ref, outs, held, i * 384)


def slab_kernel(base, *refs):
    pieces, slab = refs[:-1], refs[-1]
    n = len(pieces)
    for m, piece in enumerate(pieces):
        for h in range(OWN):
            for sp in range(4):
                row, to = base + h * 128 + sp * 32, (h * n + m) * 32
                slab[to : to + 32, sp * 128 : sp * 128 + 128] = piece[row : row + 32, :]


def logits_kernel(*refs):
    pieces, slabs = refs[:4], refs[4:-5]
    own, others, held = refs[-5], refs[-4:-1], refs[-1]
    me = lax.axis_index("x")
    for m, piece in enumerate(pieces):
        at = lax.rem(m - me + 4, 4)
        for h in range(OWN):
            for sp in range(4):
                row = h * 128 + sp * 32
                held[h, at, :, sp * 128 : sp * 128 + 128] = piece[row : row + 32, :]
    for h in range(OWN):
        query = held[h].reshape(128, 512)
        for j in range(len(slabs) // 2):
            keys = jnp.concatenate(
                [slab[h * 128 : h * 128 + 128, :] for slab in slabs[2 * j : 2 * j + 2]], axis=0
            )
            part = lax.dot_general(
                query, keys, (((1,), (1,)), ((), ())), preferred_element_type=F32
            )
            cols = slice(j * 256, j * 256 + 256)
            own[h * 32 : h * 32 + 32, cols] = part[:32]
            for k, out in enumerate(others):
                out[h * 32 : h * 32 + 32, cols] = part[k * 32 + 32 : k * 32 + 64].astype(BF16)


def sum_kernel(own, r1, r2, r3, total, sent):
    s = own[...] + r1[...].astype(F32) + r2[...].astype(F32) + r3[...].astype(F32)
    total[...] = s
    sent[...] = s.astype(BF16)


def softmax_kernel(scale, total, other, probs):
    logits = (total[...] + other[...].astype(F32)) * scale
    top = jnp.max(logits, axis=-1, keepdims=True)
    e = jnp.exp(logits - top)
    probs[...] = (e / jnp.sum(e, axis=-1, keepdims=True)).astype(BF16)


def context_kernel(*refs):
    probs, slabs, outs, held = refs[:4], refs[4:-5], refs[-5:-1], refs[-1]
    me = lax.axis_index("x")
    for k, piece in enumerate(probs):
        at = lax.rem(me - k + 4, 4)
        for h in range(OWN):
            held[h, at] = piece[h * 32 : h * 32 + 32, :]
    for h in range(OWN):
        p = held[h].reshape(128, 1024)
        total = None
        for j in range(4):
            values = jnp.concatenate(
                [slab[h * 128 : h * 128 + 128, :] for slab in slabs[2 * j : 2 * j + 2]], axis=0
            )
            part = jnp.dot(
                p[:, j * 256 : j * 256 + 256], values, preferred_element_type=F32
            )
            total = part if total is None else total + part
        total = total.astype(BF16)
        for m, out in enumerate(outs):
            for sp in range(4):
                row = h * 128 + sp * 32
                out[row : row + 32, :] = total[
                    m * 32 : m * 32 + 32, sp * 128 : sp * 128 + 128
                ]


def out_kernel(c0, c1, c2, c3, x_ref, w_ref, out, held, context):
    me = lax.axis_index("zl")
    for m, piece in enumerate((c0, c1, c2, c3)):
        held[jnp.bitwise_xor(me, m)] = piece[...]

    def block(h):
        return held[h // OWN, (h % OWN) * 128 : (h % OWN) * 128 + 128, :].astype(F32)

    for n in range(HEADS // 2):
        a, b = block(2 * n), block(2 * n + 1)
        even = jnp.concatenate([a[:, :64], b[:, :64]], axis=1).astype(BF16)
        odd = jnp.concatenate([a[:, 64:], b[:, 64:]], axis=1).astype(BF16)
        for sp in range(4):
            rows = slice(sp * 32, sp * 32 + 32)
            cols = slice(n * 128, n * 128 + 128)
            context[sp * 64 : sp * 64 + 32, cols] = even[rows]
            context[sp * 64 + 32 : sp * 64 + 64, cols] = odd[rows]
    mixed = jnp.dot(context[...], w_ref[...], preferred_element_type=F32)
    out[...] = (x_ref[...].astype(F32) + mixed).astype(BF16)


def line(pieces):
    return (pieces[0], *(lax.ppermute(pieces[m], "zl", LINE[m]) for m in (1, 2, 3)))


def other_core(slabs):
    return [lax.ppermute(s, "c", [(0, 1), (1, 0)]) for s in slabs]


def over(axis, arrays, order=(1, 3, 2)):
    return [lax.ppermute(arrays[k], axis, RING[k]) for k in order]


def per_device(x, gain, wq, wk, wv, wf):
    flat = x.reshape(256, 768)
    piece = ((384, 128), BF16)
    part = ((96, 1024), BF16)
    whole = ((384, 512), BF16)
    weights = pltpu.VMEM((768, 768), BF16)
    pieces = pltpu.VMEM((4, 384, 128), BF16)
    normed, *keys = call(
        key_kernel,
        [((256, 768), BF16)] + [piece] * 4,
        [
            pieces,
            pltpu.VMEM((256, 768), BF16),
            pltpu.VMEM((768,), F32),
            weights,
            pltpu.SemaphoreType.DMA((3,)),
        ],
        places={0: FAR, 1: FAR, 2: FAR},
        limit=MOST,
    )(flat, gain, wk)
    keys = line(keys)

    def slab(parts, base, after=()):
        return call(functools.partial(slab_kernel, base), [whole], after=after)(*parts)[0]

    pairs = line(
        call(projection_kernel, [((768, 128), BF16)] * 4, [pieces])(normed, wq, wv)
    )
    first = slab(keys, 0)
    slabs = [first] + over("y", [first] * 4)
    slabs += other_core(slabs)
    own, *others = call(
        logits_kernel,
        [((96, 1024), F32)] + [part] * 3,
        [pltpu.VMEM((OWN, 4, 32, 512), BF16)],
    )(*pairs, *slabs)
    got = over("x", [own, *others])
    first = slab(pairs, 384)
    slabs = [first] + over("y", [first] * 4, (1, 3))
    swapped = other_core(slabs)
    last = over("y", [slab(pairs, 384, got)] * 4, (2,))
    slabs += last + swapped + other_core(last)
    total, sent = call(sum_kernel, [((96, 1024), F32), part])(own, *got)
    other = lax.ppermute(sent, "zh", [(0, 1), (1, 0)])
    scale = SIZE ** (-0.5) / (64.0**0.5)
    (probs,) = call(functools.partial(softmax_kernel, scale), [part], after=swapped)(
        total, other
    )
    probs = [probs] + over("x", [probs] * 4, (1, 2, 3))
    context = call(
        context_kernel, [piece] * 4, [pltpu.VMEM((OWN, 4, 32, 1024), BF16)]
    )(*probs, *slabs)
    (out,) = call(
        out_kernel, [((256, 768), BF16)], [pieces, pltpu.VMEM((256, 768), BF16)]
    )(*line(context), flat, wf)
    return out.reshape(8, 32, 768)


def solution(mesh):
    fine = Mesh(mesh.devices.reshape(2, 4, 4, 4, 2), ("zh", "x", "zl", "y", "c"))
    split = P(("zh", "x"), ("zl", "y", "c"), None)
    return jax.shard_map(
        per_device,
        mesh=fine,
        in_specs=(split, P(), P(), P(), P(), P()),
        out_specs=split,
        check_vma=False,
    )
```

```python
import functools

import jax
import jax.numpy as jnp
from jax import lax
from jax.experimental import pallas as pl
from jax.experimental.pallas import tpu as pltpu
from jax.sharding import Mesh
from jax.sharding import PartitionSpec as P

HEADS = 12
SIZE = 64
GROUPS = 4
OWN = HEADS // GROUPS
F32, BF16 = jnp.float32, jnp.bfloat16
LINE = [[(i, i ^ m) for i in range(4)] for m in range(4)]
RING = [[(i, (i + k) % 4) for i in range(4)] for k in range(4)]
VMEM = pl.BlockSpec(memory_space=pltpu.VMEM)
FAR = pl.BlockSpec(memory_space=pltpu.HBM)
LIMIT = 48 * 1024 * 1024


def call(body, outs, scratch=(), flops=5000000000, moved=1000000, places=None, after=()):
    def run(*args):
        count = len(args)

        def kernel(*refs):
            body(*refs[:count], *refs[count + len(after) :])

        specs = [places.get(i, VMEM) if places else VMEM for i in range(count)]
        return pl.pallas_call(
            kernel,
            out_shape=[jax.ShapeDtypeStruct(s, d) for s, d in outs],
            in_specs=specs + [FAR] * len(after),
            out_specs=[VMEM] * len(outs),
            scratch_shapes=list(scratch),
            compiler_params=pltpu.CompilerParams(vmem_limit_bytes=LIMIT),
            cost_estimate=pl.CostEstimate(
                flops=flops, bytes_accessed=moved, transcendentals=0
            ),
        )(*args, *after)

    return run


def pack(full, store):
    parts = full.reshape(4, 2, 32, HEADS * SIZE)
    even, odd = parts[:, 0].reshape(128, -1), parts[:, 1].reshape(128, -1)
    for n in range(HEADS // 2):
        a, b = even[:, n * 128 : n * 128 + 128], odd[:, n * 128 : n * 128 + 128]
        store(2 * n, jnp.concatenate([a[:, :64], b[:, :64]], axis=1).astype(BF16))
        store(2 * n + 1, jnp.concatenate([a[:, 64:], b[:, 64:]], axis=1).astype(BF16))


def key_kernel(x_far, gain_far, w_far, normed_ref, o0, o1, o2, o3, held, x_ref, gain_ref, w_ref, sems):
    copies = [
        pltpu.make_async_copy(far, near, sems.at[i])
        for i, (far, near) in enumerate(
            ((x_far, x_ref), (gain_far, gain_ref), (w_far, w_ref))
        )
    ]
    for copy in copies:
        copy.start()
    copies[0].wait()
    x = x_ref[...].astype(F32)
    mean = jnp.mean(x, axis=-1, keepdims=True)
    off = x - mean
    var = jnp.mean(off * off, axis=-1, keepdims=True)
    copies[1].wait()
    gain = gain_ref[...].reshape(1, HEADS * SIZE)
    normed = (off * lax.rsqrt(var + 1e-05) * gain).astype(BF16)
    normed_ref[...] = normed
    copies[2].wait()
    spread(normed, w_ref, (o0, o1, o2, o3), held)


def spread(normed, w_ref, outs, held, row=0):
    full = jnp.dot(normed, w_ref[...], preferred_element_type=F32)

    def store(h, block):
        held[h // OWN, (h % OWN) * 128 : (h % OWN) * 128 + 128, :] = block

    pack(full, store)
    me = lax.axis_index("zl")
    for m, out in enumerate(outs):
        out[row : row + 384, :] = held[jnp.bitwise_xor(me, m)]


def projection_kernel(normed_ref, *refs):
    n = (len(refs) - 5)
    outs, held = refs[n:-1], refs[-1]
    for i, w_ref in enumerate(refs[:n]):
        spread(normed_ref[...], w_ref, outs, held, i * 384)


def slab_kernel(base, *refs):
    pieces, slab = refs[:-1], refs[-1]
    n = len(pieces)
    for m, piece in enumerate(pieces):
        for h in range(OWN):
            for sp in range(4):
                row, to = base + h * 128 + sp * 32, (h * n + m) * 32
                slab[to : to + 32, sp * 128 : sp * 128 + 128] = piece[row : row + 32, :]


def logits_kernel(*refs):
    pieces, slabs = refs[:4], refs[4:-5]
    own, others, held = refs[-5], refs[-4:-1], refs[-1]
    me = lax.axis_index("x")
    for m, piece in enumerate(pieces):
        at = lax.rem(m - me + 4, 4)
        for h in range(OWN):
            for sp in range(4):
                row = h * 128 + sp * 32
                held[h, at, :, sp * 128 : sp * 128 + 128] = piece[row : row + 32, :]
    for h in range(OWN):
        query = held[h].reshape(128, 512)
        for j in range(len(slabs) // 2):
            keys = jnp.concatenate(
                [slab[h * 128 : h * 128 + 128, :] for slab in slabs[2 * j : 2 * j + 2]], axis=0
            )
            part = lax.dot_general(
                query, keys, (((1,), (1,)), ((), ())), preferred_element_type=F32
            )
            cols = slice(j * 256, j * 256 + 256)
            own[h * 32 : h * 32 + 32, cols] = part[:32]
            for k, out in enumerate(others):
                out[h * 32 : h * 32 + 32, cols] = part[k * 32 + 32 : k * 32 + 64].astype(BF16)


def sum_kernel(own, r1, r2, r3, total, sent):
    s = own[...] + r1[...].astype(F32) + r2[...].astype(F32) + r3[...].astype(F32)
    total[...] = s
    sent[...] = s.astype(BF16)


def copy_kernel(old, new):
    new[...] = old[...]


def softmax_kernel(scale, total, other, probs):
    logits = (total[...] + other[...].astype(F32)) * scale
    top = jnp.max(logits, axis=-1, keepdims=True)
    e = jnp.exp(logits - top)
    probs[...] = (e / jnp.sum(e, axis=-1, keepdims=True)).astype(BF16)


def context_kernel(*refs):
    probs, slabs, outs, held = refs[:4], refs[4:-5], refs[-5:-1], refs[-1]
    me = lax.axis_index("x")
    for k, piece in enumerate(probs):
        at = lax.rem(me - k + 4, 4)
        for h in range(OWN):
            held[h, at] = piece[h * 32 : h * 32 + 32, :]
    for h in range(OWN):
        p = held[h].reshape(128, 1024)
        total = None
        for j in range(4):
            values = jnp.concatenate(
                [slab[h * 128 : h * 128 + 128, :] for slab in slabs[2 * j : 2 * j + 2]], axis=0
            )
            part = jnp.dot(
                p[:, j * 256 : j * 256 + 256], values, preferred_element_type=F32
            )
            total = part if total is None else total + part
        total = total.astype(BF16)
        for m, out in enumerate(outs):
            for sp in range(4):
                row = h * 128 + sp * 32
                out[row : row + 32, :] = total[
                    m * 32 : m * 32 + 32, sp * 128 : sp * 128 + 128
                ]


def out_kernel(c0, c1, c2, c3, x_ref, w_ref, out, held, context):
    me = lax.axis_index("zl")
    for m, piece in enumerate((c0, c1, c2, c3)):
        held[jnp.bitwise_xor(me, m)] = piece[...]

    def block(h):
        return held[h // OWN, (h % OWN) * 128 : (h % OWN) * 128 + 128, :].astype(F32)

    for n in range(HEADS // 2):
        a, b = block(2 * n), block(2 * n + 1)
        even = jnp.concatenate([a[:, :64], b[:, :64]], axis=1).astype(BF16)
        odd = jnp.concatenate([a[:, 64:], b[:, 64:]], axis=1).astype(BF16)
        for sp in range(4):
            rows = slice(sp * 32, sp * 32 + 32)
            cols = slice(n * 128, n * 128 + 128)
            context[sp * 64 : sp * 64 + 32, cols] = even[rows]
            context[sp * 64 + 32 : sp * 64 + 64, cols] = odd[rows]
    mixed = jnp.dot(context[...], w_ref[...], preferred_element_type=F32)
    out[...] = (x_ref[...].astype(F32) + mixed).astype(BF16)


def line(pieces):
    return (pieces[0], *(lax.ppermute(pieces[m], "zl", LINE[m]) for m in (1, 2, 3)))


def other_core(slabs):
    return [lax.ppermute(s, "c", [(0, 1), (1, 0)]) for s in slabs]


def over(axis, arrays, order=(1, 3, 2)):
    return [lax.ppermute(arrays[k], axis, RING[k]) for k in order]


def per_device(x, gain, wq, wk, wv, wf):
    flat = x.reshape(256, 768)
    piece = ((384, 128), BF16)
    part = ((96, 1024), BF16)
    whole = ((384, 512), BF16)
    weights = pltpu.VMEM((768, 768), BF16)
    pieces = pltpu.VMEM((4, 384, 128), BF16)
    at_rest = [pltpu.with_memory_space_constraint(a, pltpu.HBM) for a in (flat, gain, wk)]
    normed, *keys = call(
        key_kernel,
        [((256, 768), BF16)] + [piece] * 4,
        [
            pieces,
            pltpu.VMEM((256, 768), BF16),
            pltpu.VMEM((768,), F32),
            weights,
            pltpu.SemaphoreType.DMA((3,)),
        ],
        places={0: FAR, 1: FAR, 2: FAR},
    )(*at_rest)
    keys = line(keys)

    def slab(parts, base, after=()):
        return call(functools.partial(slab_kernel, base), [whole], after=after)(*parts)[0]

    pairs = line(
        call(projection_kernel, [((768, 128), BF16)] * 4, [pieces])(normed, wq, wv)
    )
    first = slab(keys, 0)
    slabs = [first] + over("y", [first] * 4)
    slabs += other_core(slabs)
    own, *others = call(
        logits_kernel,
        [((96, 1024), F32)] + [part] * 3,
        [pltpu.VMEM((OWN, 4, 32, 512), BF16)],
    )(*pairs, *slabs)
    got = over("x", [own, *others])
    first = slab(pairs, 384)
    slabs = [first] + over("y", [first] * 4, (1, 3))
    swapped = other_core(slabs)
    (passed,) = call(copy_kernel, [whole], after=got)(slabs[2])
    last = over("y", [passed] * 4, (3,))
    slabs += last + swapped + other_core(last)
    total, sent = call(sum_kernel, [((96, 1024), F32), part])(own, *got)
    other = lax.ppermute(sent, "zh", [(0, 1), (1, 0)])
    scale = SIZE ** (-0.5) / (64.0**0.5)
    (probs,) = call(functools.partial(softmax_kernel, scale), [part], after=swapped)(
        total, other
    )
    probs = [probs] + over("x", [probs] * 4, (1, 2, 3))
    context = call(
        context_kernel, [piece] * 4, [pltpu.VMEM((OWN, 4, 32, 1024), BF16)]
    )(*probs, *slabs)
    (out,) = call(
        out_kernel, [((256, 768), BF16)], [pieces, pltpu.VMEM((256, 768), BF16)]
    )(*line(context), flat, wf)
    return out.reshape(8, 32, 768)


def solution(mesh):
    fine = Mesh(mesh.devices.reshape(2, 4, 4, 4, 2), ("zh", "x", "zl", "y", "c"))
    split = P(("zh", "x"), ("zl", "y", "c"), None)
    return jax.shard_map(
        per_device,
        mesh=fine,
        in_specs=(split, P(), P(), P(), P(), P()),
        out_specs=split,
        check_vma=False,
    )
```

```python
import functools

import jax
import jax.numpy as jnp
from jax import lax
from jax.experimental import pallas as pl
from jax.experimental.pallas import tpu as pltpu
from jax.sharding import Mesh
from jax.sharding import PartitionSpec as P

HEADS = 12
SIZE = 64
GROUPS = 4
OWN = HEADS // GROUPS
F32, BF16 = jnp.float32, jnp.bfloat16
LINE = [[(i, i ^ m) for i in range(4)] for m in range(4)]
RING = [[(i, (i + k) % 4) for i in range(4)] for k in range(4)]
VMEM = pl.BlockSpec(memory_space=pltpu.VMEM)
FAR = pl.BlockSpec(memory_space=pltpu.HBM)
LIMIT = 48 * 1024 * 1024


def call(body, outs, scratch=(), flops=5000000000, moved=1000000, places=None, after=()):
    def run(*args):
        count = len(args)

        def kernel(*refs):
            body(*refs[:count], *refs[count + len(after) :])

        specs = [places.get(i, VMEM) if places else VMEM for i in range(count)]
        return pl.pallas_call(
            kernel,
            out_shape=[jax.ShapeDtypeStruct(s, d) for s, d in outs],
            in_specs=specs + [FAR] * len(after),
            out_specs=[VMEM] * len(outs),
            scratch_shapes=list(scratch),
            compiler_params=pltpu.CompilerParams(vmem_limit_bytes=LIMIT),
            cost_estimate=pl.CostEstimate(
                flops=flops, bytes_accessed=moved, transcendentals=0
            ),
        )(*args, *after)

    return run


def pack(full, store):
    parts = full.astype(BF16).reshape(4, 2, 32, HEADS * SIZE)
    even, odd = parts[:, 0].reshape(128, -1), parts[:, 1].reshape(128, -1)
    for n in range(HEADS // 2):
        a, b = even[:, n * 128 : n * 128 + 128], odd[:, n * 128 : n * 128 + 128]
        store(2 * n, jnp.concatenate([a[:, :64], b[:, :64]], axis=1))
        store(2 * n + 1, jnp.concatenate([a[:, 64:], b[:, 64:]], axis=1))


def key_kernel(x_far, gain_far, w_far, normed_ref, o0, o1, o2, o3, held, x_ref, gain_ref, w_ref, sems):
    copies = [
        pltpu.make_async_copy(far, near, sems.at[i])
        for i, (far, near) in enumerate(
            ((x_far, x_ref), (gain_far, gain_ref), (w_far, w_ref))
        )
    ]
    for copy in copies:
        copy.start()
    copies[0].wait()
    x = x_ref[...].astype(F32)
    mean = jnp.mean(x, axis=-1, keepdims=True)
    off = x - mean
    var = jnp.mean(off * off, axis=-1, keepdims=True)
    copies[1].wait()
    gain = gain_ref[...].reshape(1, HEADS * SIZE)
    normed = (off * lax.rsqrt(var + 1e-05) * gain).astype(BF16)
    normed_ref[...] = normed
    copies[2].wait()
    spread(normed, w_ref, (o0, o1, o2, o3), held)


def spread(normed, w_ref, outs, held, row=0):
    full = jnp.dot(normed, w_ref[...], preferred_element_type=F32)

    def store(h, block):
        held[h // OWN, (h % OWN) * 128 : (h % OWN) * 128 + 128, :] = block

    pack(full, store)
    me = lax.axis_index("zl")
    for m, out in enumerate(outs):
        out[row : row + 384, :] = held[jnp.bitwise_xor(me, m)]


def projection_kernel(normed_ref, *refs):
    n = (len(refs) - 5)
    outs, held = refs[n:-1], refs[-1]
    for i, w_ref in enumerate(refs[:n]):
        spread(normed_ref[...], w_ref, outs, held, i * 384)


def slab_kernel(base, *refs):
    pieces, slab = refs[:-1], refs[-1]
    n = len(pieces)
    for m, piece in enumerate(pieces):
        for h in range(OWN):
            for sp in range(4):
                row, to = base + h * 128 + sp * 32, (h * n + m) * 32
                slab[to : to + 32, sp * 128 : sp * 128 + 128] = piece[row : row + 32, :]


def logits_kernel(*refs):
    pieces, slabs = refs[:4], refs[4:-5]
    own, others, held = refs[-5], refs[-4:-1], refs[-1]
    me = lax.axis_index("x")
    for m, piece in enumerate(pieces):
        at = lax.rem(m - me + 4, 4)
        for h in range(OWN):
            for sp in range(4):
                row = h * 128 + sp * 32
                held[h, at, :, sp * 128 : sp * 128 + 128] = piece[row : row + 32, :]
    for h in range(OWN):
        query = held[h].reshape(128, 512)
        for j in range(len(slabs) // 2):
            keys = jnp.concatenate(
                [slab[h * 128 : h * 128 + 128, :] for slab in slabs[2 * j : 2 * j + 2]], axis=0
            )
            part = lax.dot_general(
                query, keys, (((1,), (1,)), ((), ())), preferred_element_type=F32
            )
            cols = slice(j * 256, j * 256 + 256)
            own[h * 32 : h * 32 + 32, cols] = part[:32]
            for k, out in enumerate(others):
                out[h * 32 : h * 32 + 32, cols] = part[k * 32 + 32 : k * 32 + 64].astype(BF16)


def sum_kernel(own, r1, r2, r3, total, sent):
    s = own[...] + r1[...].astype(F32) + r2[...].astype(F32) + r3[...].astype(F32)
    total[...] = s
    sent[...] = s.astype(BF16)


def copy_kernel(old, new):
    new[...] = old[...]


def softmax_kernel(scale, total, other, probs):
    logits = (total[...] + other[...].astype(F32)) * scale
    top = jnp.max(logits, axis=-1, keepdims=True)
    e = jnp.exp(logits - top)
    probs[...] = (e / jnp.sum(e, axis=-1, keepdims=True)).astype(BF16)


def context_kernel(*refs):
    probs, slabs, outs, held = refs[:4], refs[4:-5], refs[-5:-1], refs[-1]
    me = lax.axis_index("x")
    for k, piece in enumerate(probs):
        at = lax.rem(me - k + 4, 4)
        for h in range(OWN):
            held[h, at] = piece[h * 32 : h * 32 + 32, :]
    for h in range(OWN):
        p = held[h].reshape(128, 1024)
        total = None
        for j in range(4):
            values = jnp.concatenate(
                [slab[h * 128 : h * 128 + 128, :] for slab in slabs[2 * j : 2 * j + 2]], axis=0
            )
            part = jnp.dot(
                p[:, j * 256 : j * 256 + 256], values, preferred_element_type=F32
            )
            total = part if total is None else total + part
        total = total.astype(BF16)
        for m, out in enumerate(outs):
            for sp in range(4):
                row = h * 128 + sp * 32
                out[row : row + 32, :] = total[
                    m * 32 : m * 32 + 32, sp * 128 : sp * 128 + 128
                ]


def out_kernel(c0, c1, c2, c3, x_ref, w_ref, out, held, context):
    me = lax.axis_index("zl")
    for m, piece in enumerate((c0, c1, c2, c3)):
        held[jnp.bitwise_xor(me, m)] = piece[...]

    def block(h):
        return held[h // OWN, (h % OWN) * 128 : (h % OWN) * 128 + 128, :]

    for n in range(HEADS // 2):
        a, b = block(2 * n), block(2 * n + 1)
        even = jnp.concatenate([a[:, :64], b[:, :64]], axis=1)
        odd = jnp.concatenate([a[:, 64:], b[:, 64:]], axis=1)
        for sp in range(4):
            rows = slice(sp * 32, sp * 32 + 32)
            cols = slice(n * 128, n * 128 + 128)
            context[sp * 64 : sp * 64 + 32, cols] = even[rows]
            context[sp * 64 + 32 : sp * 64 + 64, cols] = odd[rows]
    mixed = jnp.dot(context[...], w_ref[...], preferred_element_type=F32)
    out[...] = (x_ref[...].astype(F32) + mixed).astype(BF16)


def line(pieces, order=(1, 2, 3)):
    got = {m: lax.ppermute(pieces[m], "zl", LINE[m]) for m in order}
    return (pieces[0], got[1], got[2], got[3])


def other_core(slabs):
    return [lax.ppermute(s, "c", [(0, 1), (1, 0)]) for s in slabs]


def over(axis, arrays, order=(1, 3, 2)):
    return [lax.ppermute(arrays[k], axis, RING[k]) for k in order]


def per_device(x, gain, wq, wk, wv, wf):
    flat = x.reshape(256, 768)
    piece = ((384, 128), BF16)
    part = ((96, 1024), BF16)
    whole = ((384, 512), BF16)
    weights = pltpu.VMEM((768, 768), BF16)
    pieces = pltpu.VMEM((4, 384, 128), BF16)
    at_rest = [pltpu.with_memory_space_constraint(a, pltpu.HBM) for a in (flat, gain, wk)]
    normed, *keys = call(
        key_kernel,
        [((256, 768), BF16)] + [piece] * 4,
        [
            pieces,
            pltpu.VMEM((256, 768), BF16),
            pltpu.VMEM((768,), F32),
            weights,
            pltpu.SemaphoreType.DMA((3,)),
        ],
        places={0: FAR, 1: FAR, 2: FAR},
    )(*at_rest)
    keys = line(keys, (3, 2, 1))

    def slab(parts, base, after=()):
        return call(functools.partial(slab_kernel, base), [whole], after=after)(*parts)[0]

    pairs = line(
        call(projection_kernel, [((768, 128), BF16)] * 4, [pieces])(normed, wq, wv)
    )
    first = slab(keys, 0)
    slabs = [first] + over("y", [first] * 4)
    slabs += other_core(slabs)
    own, *others = call(
        logits_kernel,
        [((96, 1024), F32)] + [part] * 3,
        [pltpu.VMEM((OWN, 4, 32, 512), BF16)],
    )(*pairs, *slabs)
    got = over("x", [own, *others])
    first = slab(pairs, 384)
    slabs = [first] + over("y", [first] * 4, (1, 3))
    swapped = other_core(slabs)
    (passed,) = call(copy_kernel, [whole], after=got)(slabs[2])
    last = over("y", [passed] * 4, (3,))
    slabs += last + swapped + other_core(last)
    total, sent = call(sum_kernel, [((96, 1024), F32), part])(own, *got)
    other = lax.ppermute(sent, "zh", [(0, 1), (1, 0)])
    scale = SIZE ** (-0.5) / (64.0**0.5)
    (probs,) = call(functools.partial(softmax_kernel, scale), [part], after=swapped)(
        total, other
    )
    near, back, far = over("x", [probs] * 4, (1, 3, 2))
    probs = [probs, near, far, back]
    context = call(
        context_kernel, [piece] * 4, [pltpu.VMEM((OWN, 4, 32, 1024), BF16)]
    )(*probs, *slabs)
    (out,) = call(
        out_kernel, [((256, 768), BF16)], [pieces, pltpu.VMEM((256, 768), BF16)]
    )(*line(context), flat, wf)
    return out.reshape(8, 32, 768)


def solution(mesh):
    fine = Mesh(mesh.devices.reshape(2, 4, 4, 4, 2), ("zh", "x", "zl", "y", "c"))
    split = P(("zh", "x"), ("zl", "y", "c"), None)
    return jax.shard_map(
        per_device,
        mesh=fine,
        in_specs=(split, P(), P(), P(), P(), P()),
        out_specs=split,
        check_vma=False,
    )
```

```python
import functools

import jax
import jax.numpy as jnp
from jax import lax
from jax.experimental import pallas as pl
from jax.experimental.pallas import tpu as pltpu
from jax.sharding import Mesh
from jax.sharding import PartitionSpec as P

HEADS = 12
SIZE = 64
GROUPS = 4
OWN = HEADS // GROUPS
F32, BF16 = jnp.float32, jnp.bfloat16
LINE = [[(i, i ^ m) for i in range(4)] for m in range(4)]
RING = [[(i, (i + k) % 4) for i in range(4)] for k in range(4)]
VMEM = pl.BlockSpec(memory_space=pltpu.VMEM)
FAR = pl.BlockSpec(memory_space=pltpu.HBM)
LIMIT = 48 * 1024 * 1024


def call(body, outs, scratch=(), flops=5000000000, moved=1000000, places=None, after=()):
    def run(*args):
        count = len(args)

        def kernel(*refs):
            body(*refs[:count], *refs[count + len(after) :])

        specs = [places.get(i, VMEM) if places else VMEM for i in range(count)]
        return pl.pallas_call(
            kernel,
            out_shape=[jax.ShapeDtypeStruct(s, d) for s, d in outs],
            in_specs=specs + [FAR] * len(after),
            out_specs=[VMEM] * len(outs),
            scratch_shapes=list(scratch),
            compiler_params=pltpu.CompilerParams(vmem_limit_bytes=LIMIT),
            cost_estimate=pl.CostEstimate(
                flops=flops, bytes_accessed=moved, transcendentals=0
            ),
        )(*args, *after)

    return run


def pack(full, store):
    parts = full.astype(BF16).reshape(4, 2, 32, HEADS * SIZE)
    even, odd = parts[:, 0].reshape(128, -1), parts[:, 1].reshape(128, -1)
    for n in range(HEADS // 2):
        a, b = even[:, n * 128 : n * 128 + 128], odd[:, n * 128 : n * 128 + 128]
        store(2 * n, jnp.concatenate([a[:, :64], b[:, :64]], axis=1))
        store(2 * n + 1, jnp.concatenate([a[:, 64:], b[:, 64:]], axis=1))


def key_kernel(x_far, gain_far, w_far, normed_ref, o0, o1, o2, o3, held, x_ref, gain_ref, w_ref, sems):
    copies = [
        pltpu.make_async_copy(far, near, sems.at[i])
        for i, (far, near) in enumerate(
            ((x_far, x_ref), (gain_far, gain_ref), (w_far, w_ref))
        )
    ]
    for copy in copies:
        copy.start()
    copies[0].wait()
    x = x_ref[...].astype(F32)
    mean = jnp.mean(x, axis=-1, keepdims=True)
    off = x - mean
    var = jnp.mean(off * off, axis=-1, keepdims=True)
    copies[1].wait()
    gain = gain_ref[...].reshape(1, HEADS * SIZE)
    normed = (off * lax.rsqrt(var + 1e-05) * gain).astype(BF16)
    normed_ref[...] = normed
    copies[2].wait()
    spread(normed, w_ref, (o0, o1, o2, o3), held)


def spread(normed, w_ref, outs, held, row=0):
    full = jnp.dot(normed, w_ref[...], preferred_element_type=F32)

    def store(h, block):
        held[h // OWN, (h % OWN) * 128 : (h % OWN) * 128 + 128, :] = block

    pack(full, store)
    me = lax.axis_index("zl")
    for m, out in enumerate(outs):
        out[row : row + 384, :] = held[jnp.bitwise_xor(me, m)]


def projection_kernel(normed_ref, *refs):
    n = (len(refs) - 5)
    outs, held = refs[n:-1], refs[-1]
    for i, w_ref in enumerate(refs[:n]):
        spread(normed_ref[...], w_ref, outs, held, i * 384)


def slab_kernel(base, *refs):
    pieces, slab = refs[:-1], refs[-1]
    n = len(pieces)
    for m, piece in enumerate(pieces):
        for h in range(OWN):
            for sp in range(4):
                row, to = base + h * 128 + sp * 32, (h * n + m) * 32
                slab[to : to + 32, sp * 128 : sp * 128 + 128] = piece[row : row + 32, :]


def logits_kernel(*refs):
    pieces, slabs = refs[:4], refs[4:-5]
    own, others, held = refs[-5], refs[-4:-1], refs[-1]
    me = lax.axis_index("x")
    for m, piece in enumerate(pieces):
        at = lax.rem(m - me + 4, 4)
        for h in range(OWN):
            for sp in range(4):
                row = h * 128 + sp * 32
                held[h, at, :, sp * 128 : sp * 128 + 128] = piece[row : row + 32, :]
    for h in range(OWN):
        query = held[h].reshape(128, 512)
        for j in range(len(slabs) // 2):
            keys = jnp.concatenate(
                [slab[h * 128 : h * 128 + 128, :] for slab in slabs[2 * j : 2 * j + 2]], axis=0
            )
            part = lax.dot_general(
                query, keys, (((1,), (1,)), ((), ())), preferred_element_type=F32
            )
            cols = slice(j * 256, j * 256 + 256)
            own[h * 32 : h * 32 + 32, cols] = part[:32]
            for k, out in enumerate(others):
                out[h * 32 : h * 32 + 32, cols] = part[k * 32 + 32 : k * 32 + 64].astype(BF16)


def sum_kernel(own, r1, r2, r3, total, sent):
    s = own[...] + r1[...].astype(F32) + r2[...].astype(F32) + r3[...].astype(F32)
    total[...] = s
    sent[...] = s.astype(BF16)


def copy_kernel(old, new):
    new[...] = old[...]


def softmax_kernel(scale, total, other, probs):
    logits = (total[...] + other[...].astype(F32)) * scale
    top = jnp.max(logits, axis=-1, keepdims=True)
    e = jnp.exp(logits - top)
    probs[...] = (e / jnp.sum(e, axis=-1, keepdims=True)).astype(BF16)


def context_kernel(*refs):
    probs, slabs, outs, held = refs[:4], refs[4:-5], refs[-5:-1], refs[-1]
    me = lax.axis_index("x")
    for k, piece in enumerate(probs):
        at = lax.rem(me - k + 4, 4)
        for h in range(OWN):
            held[h, at] = piece[h * 32 : h * 32 + 32, :]
    for h in range(OWN):
        p = held[h].reshape(128, 1024)
        total = None
        for j in range(4):
            values = jnp.concatenate(
                [slab[h * 128 : h * 128 + 128, :] for slab in slabs[2 * j : 2 * j + 2]], axis=0
            )
            part = jnp.dot(
                p[:, j * 256 : j * 256 + 256], values, preferred_element_type=F32
            )
            total = part if total is None else total + part
        total = total.astype(BF16)
        for m, out in enumerate(outs):
            for sp in range(4):
                row = h * 128 + sp * 32
                out[row : row + 32, :] = total[
                    m * 32 : m * 32 + 32, sp * 128 : sp * 128 + 128
                ]


def out_kernel(c0, c1, c2, c3, x_ref, w_ref, out, held, context):
    me = lax.axis_index("zl")
    for m, piece in enumerate((c0, c1, c2, c3)):
        held[jnp.bitwise_xor(me, m)] = piece[...]

    def block(h):
        return held[h // OWN, (h % OWN) * 128 : (h % OWN) * 128 + 128, :]

    for n in range(HEADS // 2):
        a, b = block(2 * n), block(2 * n + 1)
        even = jnp.concatenate([a[:, :64], b[:, :64]], axis=1)
        odd = jnp.concatenate([a[:, 64:], b[:, 64:]], axis=1)
        for sp in range(4):
            rows = slice(sp * 32, sp * 32 + 32)
            cols = slice(n * 128, n * 128 + 128)
            context[sp * 64 : sp * 64 + 32, cols] = even[rows]
            context[sp * 64 + 32 : sp * 64 + 64, cols] = odd[rows]
    mixed = jnp.dot(context[...], w_ref[...], preferred_element_type=F32)
    out[...] = (x_ref[...].astype(F32) + mixed).astype(BF16)


def line(pieces, order=(1, 2, 3)):
    got = {m: lax.ppermute(pieces[m], "zl", LINE[m]) for m in order}
    return (pieces[0], got[1], got[2], got[3])


def other_core(slabs):
    return [lax.ppermute(s, "c", [(0, 1), (1, 0)]) for s in slabs]


def over(axis, arrays, order=(1, 3, 2)):
    return [lax.ppermute(arrays[k], axis, RING[k]) for k in order]


def per_device(x, gain, wq, wk, wv, wf):
    flat = x.reshape(256, 768)
    piece = ((384, 128), BF16)
    part = ((96, 1024), BF16)
    whole = ((384, 512), BF16)
    weights = pltpu.VMEM((768, 768), BF16)
    pieces = pltpu.VMEM((4, 384, 128), BF16)
    at_rest = [pltpu.with_memory_space_constraint(a, pltpu.HBM) for a in (flat, gain, wk)]
    normed, *keys = call(
        key_kernel,
        [((256, 768), BF16)] + [piece] * 4,
        [
            pieces,
            pltpu.VMEM((256, 768), BF16),
            pltpu.VMEM((768,), F32),
            weights,
            pltpu.SemaphoreType.DMA((3,)),
        ],
        places={0: FAR, 1: FAR, 2: FAR},
    )(*at_rest)
    keys = line(keys, (3, 2, 1))

    def slab(parts, base, after=()):
        return call(functools.partial(slab_kernel, base), [whole], after=after)(*parts)[0]

    pairs = line(
        call(projection_kernel, [((768, 128), BF16)] * 4, [pieces])(normed, wq, wv)
    )
    first = slab(keys, 0)
    slabs = [first] + over("y", [first] * 4)
    slabs += other_core(slabs)
    own, *others = call(
        logits_kernel,
        [((96, 1024), F32)] + [part] * 3,
        [pltpu.VMEM((OWN, 4, 32, 512), BF16)],
    )(*pairs, *slabs)
    got = over("x", [own, *others])
    first = slab(pairs, 384)
    slabs = [first] + over("y", [first] * 4, (1, 3))
    swapped = other_core(slabs)
    (passed,) = call(copy_kernel, [whole], after=got)(slabs[2])
    last = over("y", [passed] * 4, (3,))
    slabs += last + swapped + other_core(last)
    total, sent = call(sum_kernel, [((96, 1024), F32), part])(own, *got)
    other = lax.ppermute(sent, "zh", [(0, 1), (1, 0)])
    scale = SIZE ** (-0.5) / (64.0**0.5)
    (probs,) = call(functools.partial(softmax_kernel, scale), [part], after=swapped)(
        total, other
    )
    near, back, far = over("x", [probs] * 4, (1, 3, 2))
    probs = [probs, near, far, back]
    context = call(
        context_kernel, [piece] * 4, [pltpu.VMEM((OWN, 4, 32, 1024), BF16)]
    )(*probs, *slabs)
    (out,) = call(
        out_kernel, [((256, 768), BF16)], [pieces, pltpu.VMEM((256, 768), BF16)]
    )(*line(context, (2, 3, 1)), flat, wf)
    return out.reshape(8, 32, 768)


def solution(mesh):
    fine = Mesh(mesh.devices.reshape(2, 4, 4, 4, 2), ("zh", "x", "zl", "y", "c"))
    split = P(("zh", "x"), ("zl", "y", "c"), None)
    return jax.shard_map(
        per_device,
        mesh=fine,
        in_specs=(split, P(), P(), P(), P(), P()),
        out_specs=split,
        check_vma=False,
    )
```
